128 devices in a mesh: row: 8 (over x, z_lo), col: 16 (over y, z_hi, core).
Axes of the slice: x: 4, y: 4, z: 4 (z_hi: 2, z_lo: 2; z = z_hi * 2 + z_lo), core: 2. Of those that a mesh axis runs over, the one named last changes fastest.
Arguments:
- features: bfloat16 [49152, 128], P(('col', 'row'))
- weight: bfloat16 [128, 128], replicated, may hold values from -0.5 to 0.5
- tiles: bfloat16 [8, 16, 864, 128, 128], P('row', 'col'), as said below
- tile_rows: int32 [8, 16, 864], P('row', 'col'), may hold values from 0 to 47, as said below
- tile_cols: int32 [8, 16, 864], P('row', 'col'), may hold values from 0 to 23
- tile_count: int32 [8, 16], P('row', 'col'), may hold values from 216 to 864, as said below
Outputs:
- aggregated: bfloat16 [49152, 128], P(('row', 'col'))
The draws below stay inside these ranges and needn't reach their ends.
Inputs may be any that keep to these rules, and one draw needn't show every extreme that they name: `tile_rows`: the slots of one block name distinct tiles of its 48 x 24 grid, padded slots included. `tile_count`: some block is full. `tiles`: nonnegative edge weights.
All inputs are finite; a program needn't handle non-finite values.
Results may differ from the reference program's by a relative error of at most 0.019.
Values may be sent and summed in bfloat16 or wider, within the bound.
A program may use at most 256 MiB of HBM per device.

```python
import jax
import jax.numpy as jnp
from jax import lax

F = 128
HID = 128
TILE = 128
GROUP = 384
NODES = 49152
TROWS = 48
TCOLS = 24
TILES_DEV = 864
N_ROW = 8
N_COL = 16


def slot_table(key):
    keys = jax.random.split(key, N_ROW * N_COL)
    picks = jax.vmap(lambda k: jax.random.permutation(k, TROWS * TCOLS)[:TILES_DEV])(keys)
    return picks.reshape(N_ROW, N_COL, TILES_DEV).astype(jnp.int32)


def draw_tile_rows(key, part):
    table = slot_table(key)
    return (table // TCOLS).astype(jnp.int32)


def draw_tile_cols(key, part):
    table = slot_table(key)
    return (table % TCOLS).astype(jnp.int32)


def draw_tile_count(key, part):
    key = jax.random.fold_in(key, 5)
    first, second = jax.random.split(key)
    counts = jax.random.randint(first, (N_ROW * N_COL,), TILES_DEV // 4, TILES_DEV + 1)
    chosen = jax.random.randint(second, (), 0, N_ROW * N_COL)
    counts = counts.at[chosen].set(TILES_DEV)
    return counts.reshape(N_ROW, N_COL).astype(jnp.int32)


def log_spread(key, shape, low, high):
    return jnp.exp(jax.random.uniform(key, shape, jnp.float32, jnp.log(low), jnp.log(high)))


def draw_tiles(key, part):
    table = slot_table(key)
    key = jax.random.fold_in(key, 11)
    first, second, third, fourth = jax.random.split(key, 4)
    block_scale = log_spread(first, (N_ROW, N_COL, 1, 1, 1), 0.1, 1.0)
    row_factor = log_spread(third, (N_ROW, TROWS, TILE), 0.01, 1.0)
    col_factor = log_spread(fourth, (N_COL, TCOLS, TILE), 0.01, 1.0)
    row_pick = row_factor[jnp.arange(N_ROW, dtype=jnp.int32)[:, None, None], table // TCOLS]
    col_pick = col_factor[jnp.arange(N_COL, dtype=jnp.int32)[None, :, None], table % TCOLS]
    base = log_spread(second, (N_ROW, N_COL, TILES_DEV, TILE, TILE), 0.01, 1.0)
    values = base * block_scale * row_pick[:, :, :, :, None] * col_pick[:, :, :, None, :]
    return values.astype(jnp.bfloat16)


def draw_features(key, part):
    key = jax.random.fold_in(key, 7)
    first, second = jax.random.split(key)
    centre = jax.random.normal(first, (NODES // GROUP, 1, F), jnp.float32)
    noise = jax.random.normal(second, (NODES // GROUP, GROUP, F), jnp.float32)
    values = centre + 0.5 * noise
    return values.reshape(NODES, F).astype(jnp.bfloat16)


def scatter_about(own_key, extent, width, bound, kind=jnp.bfloat16):
    result = jax.random.normal(own_key, extent, jnp.float32) * width
    return jnp.minimum(jnp.maximum(result, -bound), bound).astype(kind)


def setup_inputs(seed: int = 0) -> dict:
    splits = jax.random.split(jax.random.key(seed), 7)
    return {
        "features": draw_features(jax.random.fold_in(splits[6], 71), 0),
        "weight": scatter_about(splits[1], (F, HID), F ** -0.5, 0.5),
        "tiles": draw_tiles(jax.random.fold_in(splits[6], 71), 0),
        "tile_rows": draw_tile_rows(jax.random.fold_in(splits[6], 71), 0),
        "tile_cols": draw_tile_cols(jax.random.fold_in(splits[6], 71), 0),
        "tile_count": draw_tile_count(jax.random.fold_in(splits[6], 71), 0),
    }


def one_hot(index, count):
    return (index[:, None] == jnp.arange(count, dtype=jnp.int32)[None, :]).astype(jnp.float32)

def reference(features, weight, tiles, tile_rows, tile_cols, tile_count):
    flat_tiles = tiles.reshape(N_ROW * N_COL, TILES_DEV, TILE, TILE)
    flat_rows = tile_rows.reshape(N_ROW * N_COL, TILES_DEV)
    flat_cols = tile_cols.reshape(N_ROW * N_COL, TILES_DEV)
    flat_count = tile_count.reshape(N_ROW * N_COL)
    block_ids = jnp.arange(N_ROW * N_COL, dtype=jnp.int32) % N_COL

    def degrees(packed):
        w_tiles, rows, cols, count = packed
        live = (jnp.arange(TILES_DEV, dtype=jnp.int32) < count).astype(jnp.float32)
        masked = w_tiles.astype(jnp.float32) * live[:, None, None]
        row_sums = lax.optimization_barrier(jnp.sum(masked, axis=2))
        col_sums = lax.optimization_barrier(jnp.sum(masked, axis=1))
        row_part = jnp.dot(one_hot(rows, TROWS).T, row_sums, precision=lax.Precision.HIGHEST)
        col_part = jnp.dot(one_hot(cols, TCOLS).T, col_sums, precision=lax.Precision.HIGHEST)
        return (row_part.reshape(-1), col_part.reshape(-1))
    row_parts, col_parts = lax.map(degrees, (flat_tiles, flat_rows, flat_cols, flat_count))
    row_degree = 1.0 + lax.optimization_barrier(jnp.sum(row_parts.reshape(N_ROW, N_COL, N_COL * GROUP), axis=1)).reshape(NODES)
    column_degree = 1.0 + lax.optimization_barrier(jnp.sum(col_parts.reshape(N_ROW, N_COL, N_ROW * GROUP), axis=0)).reshape(NODES)
    projected = jnp.dot(features, weight, preferred_element_type=jnp.float32)
    scaled = (projected * lax.rsqrt(column_degree)[:, None]).astype(jnp.bfloat16)
    col_blocks = scaled.reshape(N_COL, TCOLS, TILE, HID)

    def products(packed):
        w_tiles, rows, cols, count, block = packed
        live = (jnp.arange(TILES_DEV, dtype=jnp.int32) < count).astype(jnp.float32)
        source = col_blocks[block][cols]
        term = jnp.einsum('tij,tjh->tih', w_tiles.astype(jnp.float32) * live[:, None, None], source.astype(jnp.float32), precision=lax.Precision.HIGHEST)
        tile_product = term.astype(jnp.bfloat16).astype(jnp.float32)
        placed = jnp.einsum('tr,tih->rih', one_hot(rows, TROWS), tile_product, precision=lax.Precision.HIGHEST)
        return placed.reshape(N_COL * GROUP, HID).astype(jnp.bfloat16)
    partial_all = lax.map(products, (flat_tiles, flat_rows, flat_cols, flat_count, block_ids))
    summed = lax.optimization_barrier(jnp.sum(partial_all.astype(jnp.float32).reshape(N_ROW, N_COL, N_COL * GROUP, HID), axis=1)).reshape(NODES, HID)
    return (summed * lax.rsqrt(row_degree)[:, None]).astype(jnp.bfloat16)
```

```python
import jax
import jax.numpy as jnp
from jax import lax
from jax.experimental import pallas as pl
from jax.experimental.pallas import tpu as pltpu
from jax.sharding import PartitionSpec as P

F32, BF16, I32 = jnp.float32, jnp.bfloat16, jnp.int32
SIDE = 128
CHUNK = 32
EXTRA = 16
HALF = 192
ORDER = ((2, 1), (1, 1), (3, 1), (2, 0), (0, 1), (1, 0), (3, 0), (0, 0))


def table(step, values):
    coef = list(values)
    for bit in (1, 2, 4):
        for i in range(8):
            if i & bit:
                coef[i] -= coef[i - bit]
    bits = (step % 2, (step // 2) % 2, step // 4)
    total = coef[0]
    for i in range(1, 8):
        if coef[i]:
            term = coef[i]
            for j in range(3):
                if i >> j & 1:
                    term = term * bits[j]
            total = total + term
    return total


def split_sums(value):
    high = value.astype(BF16)
    low = (value - high.astype(F32)).astype(BF16)
    return jnp.concatenate([high, low], axis=0)


def join_sums(value):
    return value[:8] + value[8:]


def kernel(
    n_row, n_col, slots, row_tiles, col_tiles,
    feat_hbm, weight_hbm, tiles_hbm, rows_hbm, cols_hbm, count_ref, out_hbm,
    tiles, csum, feats, weight, projected, scaled, rows_v, cols_v, slot_v, slot_s, colx,
    full, sib, from_two_lo, from_two_hi, from_lo, from_hi, from_z, out_v,
    tile_sem, local_sem, feat_send, feat_recv, colx_send, colx_recv, sib_send, sib_recv,
    y_send, y_recv, z_send, z_recv,
):
    group = feat_hbm.shape[0]
    owner_tiles = group // SIDE
    step_tiles = 2 * owner_tiles
    row = lax.axis_index("row")
    col = lax.axis_index("col")
    core = col % 2
    z_hi = (col // 2) % 2
    y = col // 4
    sibling = (row, col + 1 - 2 * core)
    y_next = (row, ((y + 1) % 4) * 4 + col % 4)
    y_prev = (row, ((y + 3) % 4) * 4 + col % 4)
    z_other = (row, y * 4 + (1 - z_hi) * 2 + core)
    row_peers = [((row + i) % n_row, col) for i in range(1, n_row)]

    def tile_copy(k):
        part = pl.ds(k * CHUNK, CHUNK)
        return pltpu.make_async_copy(tiles_hbm.at[part], tiles.at[part], tile_sem.at[k])

    def send(src, dst, send_sem, recv_sem, device):
        return pltpu.make_async_remote_copy(
            src_ref=src, dst_ref=dst, send_sem=send_sem, recv_sem=recv_sem,
            device_id=device, device_id_type=pl.DeviceIdType.MESH,
        )

    chunks = slots // CHUNK
    local = [
        pltpu.make_async_copy(cols_hbm, cols_v, local_sem.at[0]),
        pltpu.make_async_copy(rows_hbm, rows_v, local_sem.at[1]),
        pltpu.make_async_copy(weight_hbm, weight, local_sem.at[2]),
        pltpu.make_async_copy(feat_hbm, feats.at[row], local_sem.at[3]),
    ]
    for copy in local:
        copy.start()
    for k in range(chunks):
        tile_copy(k).start()

    barrier = pltpu.get_barrier_semaphore()
    partners = row_peers + [sibling, y_next, y_prev, z_other]
    for device in partners:
        pl.semaphore_signal(barrier, inc=1, device_id=device, device_id_type=pl.DeviceIdType.MESH)
    pl.semaphore_wait(barrier, len(partners))

    feat_copies = [
        send(feat_hbm, feats.at[row], feat_send.at[i], feat_recv.at[i], device)
        for i, device in enumerate(row_peers)
    ]
    for copy in feat_copies:
        copy.start()

    tiles[slots] = jnp.zeros((SIDE, SIDE), BF16)
    scaled[:, SIDE:] = jnp.ones((col_tiles * SIDE, SIDE), BF16)
    count = count_ref[0, 0]
    sublane = lax.broadcasted_iota(I32, (8, SIDE), 0)

    def column_sums(k, carry):
        tile_copy(k).wait()
        for g in range(CHUNK // 8):
            first = k * CHUNK + g * 8
            sums = None
            for s in range(8):
                tile = tiles[first + s].astype(F32)
                part = jnp.sum(tile.reshape(SIDE // 8, 8, SIDE), axis=0)
                part = jnp.broadcast_to(jnp.sum(part, axis=0, keepdims=True), (8, SIDE))
                sums = part if s == 0 else jnp.where(sublane == s, part, sums)
            live = first + sublane < count
            csum[pl.ds(pl.multiple_of(first, 8), 8), :] = jnp.where(live, sums, 0.0)
        return carry

    lax.fori_loop(0, chunks // 2, column_sums, 0)

    for copy in local:
        copy.wait()
    lane = lax.broadcasted_iota(I32, (1, slots), 1)
    place = jnp.where(lane < count, rows_v[...] * 32 + cols_v[...], -1)
    padded = jnp.concatenate([place, jnp.full((1, 7 * SIDE - slots), -1, I32)], axis=1)
    stacked = jnp.concatenate(
        [padded[:, g * SIDE:(g + 1) * SIDE] for g in range(7)] + [jnp.full((SIDE - 7, SIDE), -1, I32)], axis=0
    )
    turned = stacked.T
    places = [jnp.broadcast_to(turned[:, g:g + 1], (SIDE, SIDE)) for g in range(7)]
    slot_id = lax.broadcasted_iota(I32, (SIDE, SIDE), 0)
    lane_id = lax.broadcasted_iota(I32, (SIDE, SIDE), 1)
    slot_v[...] = jnp.full(slot_v.shape, slots, I32)
    for b in range(row_tiles * 32 // SIDE):
        best = jnp.full((SIDE, SIDE), slots, I32)
        for g in range(7):
            best = jnp.where(places[g] == lane_id + b * SIDE, slot_id + g * SIDE, best)
        slot_v[b:b + 1, :] = jnp.min(best, axis=0, keepdims=True)
    to_scalar = pltpu.make_async_copy(slot_v, slot_s, local_sem.at[4])
    to_scalar.start()

    for copy in feat_copies:
        copy.wait_recv()
    for j in range(n_row):
        projected[pl.ds(j * group, group), :] = jnp.dot(
            feats[j], weight[...], preferred_element_type=F32
        )
    to_scalar.wait()

    lax.fori_loop(chunks // 2, chunks, column_sums, 0)

    kind = lax.broadcasted_iota(I32, (col_tiles, slots), 0)
    at = lax.broadcasted_iota(I32, (col_tiles, slots), 1)
    pick = jnp.where((kind == cols_v[...]) & (at < count), 1.0, 0.0).astype(BF16)
    rest = csum[...]
    own = jnp.zeros((col_tiles, SIDE), F32)
    for _ in range(3):
        piece = rest.astype(BF16)
        own = own + jnp.dot(pick, piece, preferred_element_type=F32)
        rest = rest - piece.astype(F32)
    colx[row] = own
    colx_copies = [
        send(colx.at[row], colx.at[row], colx_send.at[i], colx_recv.at[i], device)
        for i, device in enumerate(row_peers)
    ]
    for copy in colx_copies:
        copy.start()
    for copy in colx_copies:
        copy.wait_recv()
    degree = colx[0]
    for j in range(1, n_row):
        degree = degree + colx[j]
    factor = lax.rsqrt(1.0 + degree)
    factor = jnp.concatenate([factor, jnp.ones((SIDE - col_tiles, SIDE), F32)], axis=0).T
    for c in range(col_tiles):
        block = projected[c * SIDE:(c + 1) * SIDE, :] * factor[:, c:c + 1]
        scaled[c * SIDE:(c + 1) * SIDE, :SIDE] = block.astype(BF16)

    eye = jnp.where(slot_id == lane_id, 1.0, 0.0)

    def sib_copy(k):
        return send(full.at[k, 1 - core], sib.at[k], sib_send.at[k], sib_recv.at[k], sibling)

    low, high = pl.ds(0, HALF), pl.ds(HALF, group + EXTRA - HALF)

    def two_copies(k, dz):
        return (
            send(full.at[k, core, low], from_two_lo.at[dz], y_send.at[4 * dz], y_recv.at[4 * dz], y_next),
            send(full.at[k, core, high], from_two_hi.at[dz], y_send.at[4 * dz + 1], y_recv.at[4 * dz + 1], y_prev),
        )

    def lo_copy(k, dz):
        return send(full.at[k, core], from_lo.at[dz], y_send.at[4 * dz + 2], y_recv.at[4 * dz + 2], y_next)

    def hi_copy(k, dz):
        return send(full.at[k, core], from_hi.at[dz], y_send.at[4 * dz + 3], y_recv.at[4 * dz + 3], y_prev)

    def z_copy(k):
        return send(full.at[k, core], from_z, z_send, z_recv, z_other)

    def add_up(k, others):
        total = full[k, core].astype(F32) + sib[k].astype(F32)
        for other in others:
            total = total + other[...].astype(F32)
        return total

    def keep(k, total):
        full[k, core, pl.ds(0, group), :] = total[:group].astype(BF16)
        full[k, core, pl.ds(group, EXTRA), :] = split_sums(join_sums(total[group:]))

    index = {pair: k for k, pair in enumerate(ORDER)}

    def pass_on(k):
        dy, dz = ORDER[k]
        sib_copy(k).wait_recv()
        if dy == 2:
            keep(k, add_up(k, []))
            for copy in two_copies(k, dz):
                copy.start()
        elif dy == 1:
            two_copies(index[2, dz], dz)[0].wait_recv()
            total = add_up(k, [])
            top = total[:HALF] + from_two_lo[dz].astype(F32)
            keep(k, jnp.concatenate([top, total[HALF:]], axis=0))
            lo_copy(k, dz).start()
        elif dy == 3:
            two_copies(index[2, dz], dz)[1].wait_recv()
            total = add_up(k, [])
            bottom = total[HALF:] + from_two_hi[dz].astype(F32)
            keep(k, jnp.concatenate([total[:HALF], bottom], axis=0))
            hi_copy(k, dz).start()
        elif dz == 1:
            lo_copy(index[1, 1], 1).wait_recv()
            hi_copy(index[3, 1], 1).wait_recv()
            keep(k, add_up(k, [from_lo.at[1], from_hi.at[1]]))
            z_copy(k).start()

    def product(k, carry):
        chip = ((y + table(k, [d[0] for d in ORDER])) % 4) * 2 + (z_hi + table(k, [d[1] for d in ORDER])) % 2
        first = chip * step_tiles
        wide = []
        for a in range(step_tiles):
            at_row = first + a
            wide.append(jnp.concatenate(
                [tiles[slot_s[at_row // 4, (at_row % 4) * 32 + c]] for c in range(col_tiles)], axis=1
            ))
        result = jnp.dot(jnp.concatenate(wide, axis=0), scaled[...], preferred_element_type=F32)
        for h in range(2):
            part = result[h * group:(h + 1) * group]
            full[k, h, pl.ds(0, group), :] = part[:, :SIDE].astype(BF16)
            sums = [
                jnp.sum(part[i * SIDE:(i + 1) * SIDE, SIDE:] * eye, axis=0, keepdims=True)
                for i in range(owner_tiles)
            ]
            sums.append(jnp.zeros((8 - owner_tiles, SIDE), F32))
            full[k, h, pl.ds(group, EXTRA), :] = split_sums(jnp.concatenate(sums, axis=0))
        sib_copy(k).start()
        for done in range(7):
            @pl.when(k == done + 1)
            def _():
                pass_on(done)
        return carry

    lax.fori_loop(0, 8, product, 0)

    last = index[0, 0]
    sib_copy(last).wait_recv()
    lo_copy(index[1, 0], 0).wait_recv()
    hi_copy(index[3, 0], 0).wait_recv()
    z_copy(index[0, 1]).wait_recv()
    total = add_up(last, [from_lo.at[0], from_hi.at[0], from_z])
    norm = lax.rsqrt(1.0 + join_sums(total[group:]))
    norm = jnp.concatenate([norm, jnp.ones((SIDE - 8, SIDE), F32)], axis=0).T
    for i in range(owner_tiles):
        out_v[i * SIDE:(i + 1) * SIDE, :] = (total[i * SIDE:(i + 1) * SIDE] * norm[:, i:i + 1]).astype(BF16)
    store = pltpu.make_async_copy(out_v, out_hbm, local_sem.at[5])
    store.start()

    for copy in feat_copies + colx_copies:
        copy.wait_send()
    for k, (dy, dz) in enumerate(ORDER):
        sib_copy(k).wait_send()
        if dy == 2:
            for copy in two_copies(k, dz):
                copy.wait_send()
        elif dy == 1:
            lo_copy(k, dz).wait_send()
        elif dy == 3:
            hi_copy(k, dz).wait_send()
        elif dz == 1:
            z_copy(k).wait_send()
    store.wait()


def body(features, weight, tiles, tile_rows, tile_cols, tile_count):
    n_row, n_col = lax.axis_size("row"), lax.axis_size("col")
    group, width = features.shape
    hidden = weight.shape[1]
    slots, side = tiles.shape[2], tiles.shape[3]
    row_tiles = n_col * group // side
    col_tiles = n_row * group // side
    block = group + EXTRA
    dma = pltpu.SemaphoreType.DMA

    def run(*refs):
        kernel(n_row, n_col, slots, row_tiles, col_tiles, *refs)

    anywhere = pl.BlockSpec(memory_space=pl.ANY)
    return pl.pallas_call(
        run,
        out_shape=jax.ShapeDtypeStruct((group, hidden), BF16),
        in_specs=[anywhere] * 5 + [pl.BlockSpec(memory_space=pltpu.SMEM)],
        out_specs=anywhere,
        scratch_shapes=[
            pltpu.VMEM((slots + 1, side, side), BF16),
            pltpu.VMEM((slots, side), F32),
            pltpu.VMEM((n_row, group, width), BF16),
            pltpu.VMEM((width, hidden), BF16),
            pltpu.VMEM((col_tiles * side, hidden), F32),
            pltpu.VMEM((col_tiles * side, 2 * hidden), BF16),
            pltpu.VMEM((1, slots), I32),
            pltpu.VMEM((1, slots), I32),
            pltpu.VMEM((16, side), I32),
            pltpu.SMEM((16, side), I32),
            pltpu.VMEM((n_row, col_tiles, side), F32),
            pltpu.VMEM((8, 2, block, hidden), BF16),
            pltpu.VMEM((8, block, hidden), BF16),
            pltpu.VMEM((2, HALF, hidden), BF16),
            pltpu.VMEM((2, block - HALF, hidden), BF16),
            pltpu.VMEM((2, block, hidden), BF16),
            pltpu.VMEM((2, block, hidden), BF16),
            pltpu.VMEM((block, hidden), BF16),
            pltpu.VMEM((group, hidden), BF16),
            dma((slots // CHUNK,)),
            dma((6,)),
            dma((n_row - 1,)),
            dma((n_row - 1,)),
            dma((n_row - 1,)),
            dma((n_row - 1,)),
            dma((8,)),
            dma((8,)),
            dma((8,)),
            dma((8,)),
            dma,
            dma,
        ],
        compiler_params=pltpu.CompilerParams(
            collective_id=0, has_side_effects=True, vmem_limit_bytes=56 * 2**20
        ),
    )(
        features, weight, tiles.reshape(slots, side, side),
        tile_rows.reshape(1, slots), tile_cols.reshape(1, slots), tile_count.reshape(1, 1),
    )


def solution(mesh):
    in_specs = (
        P(("col", "row"), None),
        P(),
        P("row", "col", None, None, None),
        P("row", "col", None),
        P("row", "col", None),
        P("row", "col"),
    )
    out_specs = P(("row", "col"), None)
    return jax.shard_map(body, mesh=mesh, in_specs=in_specs, out_specs=out_specs, check_vma=False)
```

```python
import jax
import jax.numpy as jnp
from jax import lax
from jax.experimental import pallas as pl
from jax.experimental.pallas import tpu as pltpu
from jax.sharding import PartitionSpec as P

F32, BF16, I32 = jnp.float32, jnp.bfloat16, jnp.int32
SIDE = 128
CHUNK = 32
EXTRA = 16
FIRST = 3
AHEAD = 10
ORDER = ((2, 1), (1, 1), (3, 1), (2, 0), (0, 1), (1, 0), (3, 0), (0, 0))


def table(step, values):
    coef = list(values)
    for bit in (1, 2, 4):
        for i in range(8):
            if i & bit:
                coef[i] -= coef[i - bit]
    bits = (step % 2, (step // 2) % 2, step // 4)
    total = coef[0]
    for i in range(1, 8):
        if coef[i]:
            term = coef[i]
            for j in range(3):
                if i >> j & 1:
                    term = term * bits[j]
            total = total + term
    return total


def split_sums(value):
    high = value.astype(BF16)
    low = (value - high.astype(F32)).astype(BF16)
    return jnp.concatenate([high, low], axis=0)


def join_sums(value):
    return value[:8] + value[8:]


def kernel(
    n_row, n_col, slots, row_tiles, col_tiles,
    feat_hbm, weight_hbm, tiles_hbm, rows_hbm, cols_hbm, count_hbm, out_ref,
    tiles, csum, count_s, feats, weight, projected, scaled, rows_v, cols_v, slot_v, slot_s, colx,
    full, sib, land,
    tile_sem, local_sem, feat_send, feat_recv, colx_send, colx_recv, sib_send, sib_recv,
    own_send, own_recv, y_two, z_one, z_two,
):
    group = feat_hbm.shape[0]
    owner_tiles = group // SIDE
    step_tiles = 2 * owner_tiles
    row = lax.axis_index("row")
    col = lax.axis_index("col")
    core = col % 2
    z_hi = (col // 2) % 2
    y = col // 4
    sibling = (row, col + 1 - 2 * core)

    def chip_peer(dy, dz):
        return (row, (((y + dy) % 4) * 2 + (z_hi + dz) % 2) * 2 + core)

    row_peers = [((row + i) % n_row, col) for i in range(1, n_row)]

    def tile_copy(k):
        part = pl.ds(k * CHUNK, CHUNK)
        return pltpu.make_async_copy(tiles_hbm.at[part], tiles.at[part], tile_sem.at[k])

    def send(src, dst, send_sem, recv_sem, device):
        return pltpu.make_async_remote_copy(
            src_ref=src, dst_ref=dst, send_sem=send_sem, recv_sem=recv_sem,
            device_id=device, device_id_type=pl.DeviceIdType.MESH,
        )

    chunks = slots // CHUNK
    local = [
        pltpu.make_async_copy(cols_hbm, cols_v, local_sem.at[0]),
        pltpu.make_async_copy(rows_hbm, rows_v, local_sem.at[1]),
        pltpu.make_async_copy(weight_hbm, weight, local_sem.at[2]),
        pltpu.make_async_copy(feat_hbm, feats.at[row], local_sem.at[3]),
        pltpu.make_async_copy(count_hbm, count_s, local_sem.at[5]),
    ]
    for k in range(FIRST):
        tile_copy(k).start()
    for copy in local:
        copy.start()
    barrier = pltpu.get_barrier_semaphore()
    owners = [chip_peer(dy, dz) for dy, dz in ORDER[:-1]]
    y_next, y_prev, z_other = chip_peer(1, 0), chip_peer(3, 0), chip_peer(0, 1)
    partners = row_peers + [sibling, y_next, y_prev, z_other]
    for device in partners:
        pl.semaphore_signal(barrier, inc=1, device_id=device, device_id_type=pl.DeviceIdType.MESH)
    for k in range(FIRST, AHEAD):
        tile_copy(k).start()
    pl.semaphore_wait(barrier, len(partners))
    feat_copies = [
        send(feat_hbm, feats.at[row], feat_send.at[i], feat_recv.at[i], device)
        for i, device in enumerate(row_peers)
    ]
    for copy in feat_copies:
        copy.start()
    for k in range(AHEAD, chunks):
        tile_copy(k).start()

    def tell(sem, device):
        pl.semaphore_signal(sem, inc=1, device_id=device, device_id_type=pl.DeviceIdType.MESH)

    tell(y_two, y_prev)
    tell(z_one, z_other)

    tiles[slots] = jnp.zeros((SIDE, SIDE), BF16)
    scaled[:, SIDE:] = jnp.ones((col_tiles * SIDE, SIDE), BF16)
    sublane = lax.broadcasted_iota(I32, (8, SIDE), 0)

    def slot_sums(k, carry):
        tile_copy(k).wait()
        for g in range(CHUNK // 8):
            first = k * CHUNK + g * 8
            sums = None
            for s in range(8):
                tile = tiles[first + s].astype(F32)
                part = jnp.sum(tile.reshape(SIDE // 8, 8, SIDE), axis=0)
                part = jnp.broadcast_to(jnp.sum(part, axis=0, keepdims=True), (8, SIDE))
                sums = part if s == 0 else jnp.where(sublane == s, part, sums)
            csum[pl.ds(pl.multiple_of(first, 8), 8), :] = sums
        return carry

    def column_sums(first, end):
        size = end - first
        kind = lax.broadcasted_iota(I32, (col_tiles, size), 0)
        at = lax.broadcasted_iota(I32, (col_tiles, size), 1) + first
        pick = jnp.where((kind == cols_v[:, first:end]) & (at < count), 1.0, 0.0).astype(BF16)
        live = lax.broadcasted_iota(I32, (size, SIDE), 0) + first < count
        rest = jnp.where(live, csum[first:end], 0.0)
        total = jnp.zeros((col_tiles, SIDE), F32)
        for _ in range(3):
            piece = rest.astype(BF16)
            total = total + jnp.dot(pick, piece, preferred_element_type=F32)
            rest = rest - piece.astype(F32)
        return total

    late = (slots - 1) // SIDE * SIDE
    lax.fori_loop(0, 12, slot_sums, 0)

    for copy in local:
        copy.wait()
    count = count_s[0, 0]
    lane = lax.broadcasted_iota(I32, (1, slots), 1)
    place = jnp.where(lane < count, rows_v[...] * 32 + cols_v[...], -1)
    padded = jnp.concatenate([place, jnp.full((1, 7 * SIDE - slots), -1, I32)], axis=1)
    stacked = jnp.concatenate(
        [padded[:, g * SIDE:(g + 1) * SIDE] for g in range(7)] + [jnp.full((SIDE - 7, SIDE), -1, I32)], axis=0
    )
    turned = stacked.T
    places = [jnp.broadcast_to(turned[:, g:g + 1], (SIDE, SIDE)) for g in range(7)]
    slot_id = lax.broadcasted_iota(I32, (SIDE, SIDE), 0)
    lane_id = lax.broadcasted_iota(I32, (SIDE, SIDE), 1)
    slot_v[...] = jnp.full(slot_v.shape, slots, I32)

    def find(b, carry):
        best = jnp.full((SIDE, SIDE), slots, I32)
        for g in range(7):
            best = jnp.where(places[g] == lane_id + b * SIDE, slot_id + g * SIDE, best)
        slot_v[pl.ds(b, 1), :] = jnp.min(best, axis=0, keepdims=True)
        return carry

    lax.fori_loop(0, row_tiles * 32 // SIDE, find, 0)
    to_scalar = pltpu.make_async_copy(slot_v, slot_s, local_sem.at[4])
    to_scalar.start()


    lax.fori_loop(12, late // CHUNK, slot_sums, 0)
    own = column_sums(0, late)
    lax.fori_loop(late // CHUNK, chunks, slot_sums, 0)
    own = own + column_sums(late, slots)

    pl.semaphore_wait(y_two, 1)
    tell(z_two, z_other)

    colx[row] = own
    colx_copies = [
        send(colx.at[row], colx.at[row], colx_send.at[i], colx_recv.at[i], device)
        for i, device in enumerate(row_peers)
    ]
    for copy in colx_copies:
        copy.start()
    for copy in feat_copies:
        copy.wait_recv()

    def project(j, carry):
        projected[pl.ds(pl.multiple_of(j * group, group), group), :] = jnp.dot(
            feats[j], weight[...], preferred_element_type=F32
        )
        return carry

    lax.fori_loop(0, n_row, project, 0)
    to_scalar.wait()
    for copy in colx_copies:
        copy.wait_recv()
    degree = colx[0]
    for j in range(1, n_row):
        degree = degree + colx[j]
    factor = lax.rsqrt(1.0 + degree)
    factor = jnp.concatenate([factor, jnp.ones((SIDE - col_tiles, SIDE), F32)], axis=0).T
    for c in range(col_tiles):
        block = projected[c * SIDE:(c + 1) * SIDE, :] * factor[:, c:c + 1]
        scaled[c * SIDE:(c + 1) * SIDE, :SIDE] = block.astype(BF16)

    pl.semaphore_wait(z_one, 1)
    pl.semaphore_wait(z_two, 1)

    eye = jnp.where(slot_id == lane_id, 1.0, 0.0)

    def sib_copy(k):
        return send(full.at[k, 1 - core], sib.at[k], sib_send.at[k], sib_recv.at[k], sibling)

    def step_peer(k):
        return chip_peer(table(k, [d[0] for d in ORDER]), table(k, [d[1] for d in ORDER]))

    def owner_copy(k, device):
        return send(full.at[k, core], land.at[k], own_send.at[k], own_recv.at[k], device)

    def pair_sum(k):
        sib_copy(k).wait_recv()
        return full[k, core].astype(F32) + sib[k].astype(F32)

    def pass_on(k):
        total = pair_sum(k)
        full[k, core, pl.ds(0, group), :] = total[:group].astype(BF16)
        full[k, core, pl.ds(group, EXTRA), :] = split_sums(join_sums(total[group:]))
        owner_copy(k, step_peer(k)).start()

    def product(k, carry):
        first = (step_peer(k)[1] // 2) * step_tiles
        wide = []
        for a in range(step_tiles):
            at_row = first + a
            wide.append(jnp.concatenate(
                [tiles[slot_s[at_row // 4, (at_row % 4) * 32 + c]] for c in range(col_tiles)], axis=1
            ))
        result = jnp.dot(jnp.concatenate(wide, axis=0), scaled[...], preferred_element_type=F32)
        for h in range(2):
            part = result[h * group:(h + 1) * group]
            full[k, h, pl.ds(0, group), :] = part[:, :SIDE].astype(BF16)
            sums = [
                jnp.sum(part[i * SIDE:(i + 1) * SIDE, SIDE:] * eye, axis=0, keepdims=True)
                for i in range(owner_tiles)
            ]
            sums.append(jnp.zeros((8 - owner_tiles, SIDE), F32))
            full[k, h, pl.ds(group, EXTRA), :] = split_sums(jnp.concatenate(sums, axis=0))
        sib_copy(k).start()

        @pl.when(k > 0)
        def _():
            pass_on(k - 1)

        return carry

    lax.fori_loop(0, 8, product, 0)

    last = len(ORDER) - 1
    total = pair_sum(last)
    for k in range(last):
        owner_copy(k, owners[k]).wait_recv()
        total = total + land[k].astype(F32)
    norm = lax.rsqrt(1.0 + join_sums(total[group:]))
    norm = jnp.concatenate([norm, jnp.ones((SIDE - 8, SIDE), F32)], axis=0).T
    for i in range(owner_tiles):
        out_ref[i * SIDE:(i + 1) * SIDE, :] = (total[i * SIDE:(i + 1) * SIDE] * norm[:, i:i + 1]).astype(BF16)

    for copy in feat_copies + colx_copies:
        copy.wait_send()
    for k in range(len(ORDER)):
        sib_copy(k).wait_send()
    for k in range(last):
        owner_copy(k, owners[k]).wait_send()


def body(features, weight, tiles, tile_rows, tile_cols, tile_count):
    n_row, n_col = lax.axis_size("row"), lax.axis_size("col")
    group, width = features.shape
    hidden = weight.shape[1]
    slots, side = tiles.shape[2], tiles.shape[3]
    row_tiles = n_col * group // side
    col_tiles = n_row * group // side
    block = group + EXTRA
    dma = pltpu.SemaphoreType.DMA

    def run(*refs):
        kernel(n_row, n_col, slots, row_tiles, col_tiles, *refs)

    anywhere = pl.BlockSpec(memory_space=pl.ANY)
    return pl.pallas_call(
        run,
        out_shape=pltpu.VMEM((group, hidden), BF16),
        in_specs=[anywhere] * 5 + [pl.BlockSpec(memory_space=pltpu.HBM)],
        out_specs=pl.BlockSpec(memory_space=pltpu.VMEM),
        scratch_shapes=[
            pltpu.VMEM((slots + 1, side, side), BF16),
            pltpu.VMEM((slots, side), F32),
            pltpu.SMEM((1, 1), I32),
            pltpu.VMEM((n_row, group, width), BF16),
            pltpu.VMEM((width, hidden), BF16),
            pltpu.VMEM((col_tiles * side, hidden), F32),
            pltpu.VMEM((col_tiles * side, 2 * hidden), BF16),
            pltpu.VMEM((1, slots), I32),
            pltpu.VMEM((1, slots), I32),
            pltpu.VMEM((16, side), I32),
            pltpu.SMEM((16, side), I32),
            pltpu.VMEM((n_row, col_tiles, side), F32),
            pltpu.VMEM((8, 2, block, hidden), BF16),
            pltpu.VMEM((8, block, hidden), BF16),
            pltpu.VMEM((7, block, hidden), BF16),
            dma((slots // CHUNK,)),
            dma((6,)),
            dma((n_row - 1,)),
            dma((n_row - 1,)),
            dma((n_row - 1,)),
            dma((n_row - 1,)),
            dma((8,)),
            dma((8,)),
            dma((7,)),
            dma((7,)),
            pltpu.SemaphoreType.REGULAR,
            pltpu.SemaphoreType.REGULAR,
            pltpu.SemaphoreType.REGULAR,
        ],
        compiler_params=pltpu.CompilerParams(
            collective_id=0, has_side_effects=True, vmem_limit_bytes=56 * 2**20
        ),
    )(
        features, weight, tiles.reshape(slots, side, side),
        tile_rows.reshape(1, slots), tile_cols.reshape(1, slots), tile_count.reshape(1, 1),
    )


def solution(mesh):
    in_specs = (
        P(("col", "row"), None),
        P(),
        P("row", "col", None, None, None),
        P("row", "col", None),
        P("row", "col", None),
        P("row", "col"),
    )
    out_specs = P(("row", "col"), None)
    return jax.shard_map(body, mesh=mesh, in_specs=in_specs, out_specs=out_specs, check_vma=False)
```

```python
import jax
import jax.numpy as jnp
from jax import lax
from jax.experimental import pallas as pl
from jax.experimental.pallas import tpu as pltpu
from jax.sharding import PartitionSpec as P

F32, BF16, I32 = jnp.float32, jnp.bfloat16, jnp.int32
SIDE = 128
CHUNK = 32
EXTRA = 16
FIRST = 3
AHEAD = 10
ORDER = ((2, 1), (0, 1), (2, 0), (1, 1), (3, 1), (1, 0), (3, 0), (0, 0))


def table(step, values):
    coef = list(values)
    for bit in (1, 2, 4):
        for i in range(8):
            if i & bit:
                coef[i] -= coef[i - bit]
    bits = (step % 2, (step // 2) % 2, step // 4)
    total = coef[0]
    for i in range(1, 8):
        if coef[i]:
            term = coef[i]
            for j in range(3):
                if i >> j & 1:
                    term = term * bits[j]
            total = total + term
    return total


def split_sums(value):
    high = value.astype(BF16)
    low = (value - high.astype(F32)).astype(BF16)
    return jnp.concatenate([high, low], axis=0)


def join_sums(value):
    return value[:8] + value[8:]


def kernel(
    n_row, n_col, slots, row_tiles, col_tiles,
    feat_hbm, weight_hbm, tiles_hbm, rows_hbm, cols_hbm, count_hbm, out_ref,
    tiles, csum, count_s, feats, weight, projected, scaled, rows_v, cols_v, slot_v, slot_s, colx,
    full, sib, land,
    tile_sem, local_sem, feat_send, feat_recv, colx_send, colx_recv, sib_send, sib_recv,
    own_send, own_recv, y_two, z_one, z_two,
):
    group = feat_hbm.shape[0]
    owner_tiles = group // SIDE
    step_tiles = 2 * owner_tiles
    row = lax.axis_index("row")
    col = lax.axis_index("col")
    core = col % 2
    z_hi = (col // 2) % 2
    y = col // 4
    sibling = (row, col + 1 - 2 * core)

    def chip_peer(dy, dz):
        return (row, (((y + dy) % 4) * 2 + (z_hi + dz) % 2) * 2 + core)

    row_peers = [((row + i) % n_row, col) for i in range(1, n_row)]

    def tile_copy(k):
        part = pl.ds(k * CHUNK, CHUNK)
        return pltpu.make_async_copy(tiles_hbm.at[part], tiles.at[part], tile_sem.at[k])

    def send(src, dst, send_sem, recv_sem, device):
        return pltpu.make_async_remote_copy(
            src_ref=src, dst_ref=dst, send_sem=send_sem, recv_sem=recv_sem,
            device_id=device, device_id_type=pl.DeviceIdType.MESH,
        )

    chunks = slots // CHUNK
    local = [
        pltpu.make_async_copy(cols_hbm, cols_v, local_sem.at[0]),
        pltpu.make_async_copy(rows_hbm, rows_v, local_sem.at[1]),
        pltpu.make_async_copy(weight_hbm, weight, local_sem.at[2]),
        pltpu.make_async_copy(feat_hbm, feats.at[row], local_sem.at[3]),
        pltpu.make_async_copy(count_hbm, count_s, local_sem.at[5]),
    ]
    for k in range(FIRST):
        tile_copy(k).start()
    for copy in local:
        copy.start()
    barrier = pltpu.get_barrier_semaphore()
    owners = [chip_peer(dy, dz) for dy, dz in ORDER[:-1]]
    y_next, y_prev, z_other = chip_peer(1, 0), chip_peer(3, 0), chip_peer(0, 1)
    partners = row_peers + [sibling, y_next, y_prev, z_other]
    for device in partners:
        pl.semaphore_signal(barrier, inc=1, device_id=device, device_id_type=pl.DeviceIdType.MESH)
    for k in range(FIRST, AHEAD):
        tile_copy(k).start()
    pl.semaphore_wait(barrier, len(partners))
    feat_copies = [
        send(feat_hbm, feats.at[row], feat_send.at[i], feat_recv.at[i], device)
        for i, device in enumerate(row_peers)
    ]
    for copy in feat_copies:
        copy.start()
    for k in range(AHEAD, chunks):
        tile_copy(k).start()

    def tell(sem, device):
        pl.semaphore_signal(sem, inc=1, device_id=device, device_id_type=pl.DeviceIdType.MESH)

    tell(y_two, y_prev)
    tell(z_one, z_other)

    tiles[slots] = jnp.zeros((SIDE, SIDE), BF16)
    scaled[:, SIDE:] = jnp.ones((col_tiles * SIDE, SIDE), BF16)
    sublane = lax.broadcasted_iota(I32, (8, SIDE), 0)

    def slot_sums(k, carry):
        tile_copy(k).wait()
        for g in range(CHUNK // 8):
            first = k * CHUNK + g * 8
            sums = None
            for s in range(8):
                tile = tiles[first + s].astype(F32)
                part = jnp.sum(tile.reshape(SIDE // 8, 8, SIDE), axis=0)
                part = jnp.broadcast_to(jnp.sum(part, axis=0, keepdims=True), (8, SIDE))
                sums = part if s == 0 else jnp.where(sublane == s, part, sums)
            csum[pl.ds(pl.multiple_of(first, 8), 8), :] = sums
        return carry

    def column_sums(first, end):
        size = end - first
        kind = lax.broadcasted_iota(I32, (col_tiles, size), 0)
        at = lax.broadcasted_iota(I32, (col_tiles, size), 1) + first
        pick = jnp.where((kind == cols_v[:, first:end]) & (at < count), 1.0, 0.0).astype(BF16)
        live = lax.broadcasted_iota(I32, (size, SIDE), 0) + first < count
        rest = jnp.where(live, csum[first:end], 0.0)
        total = jnp.zeros((col_tiles, SIDE), F32)
        for _ in range(3):
            piece = rest.astype(BF16)
            total = total + jnp.dot(pick, piece, preferred_element_type=F32)
            rest = rest - piece.astype(F32)
        return total

    late = (slots - 1) // SIDE * SIDE
    lax.fori_loop(0, 12, slot_sums, 0)

    for copy in local:
        copy.wait()
    count = count_s[0, 0]
    lane = lax.broadcasted_iota(I32, (1, slots), 1)
    place = jnp.where(lane < count, rows_v[...] * 32 + cols_v[...], -1)
    padded = jnp.concatenate([place, jnp.full((1, 7 * SIDE - slots), -1, I32)], axis=1)
    stacked = jnp.concatenate(
        [padded[:, g * SIDE:(g + 1) * SIDE] for g in range(7)] + [jnp.full((SIDE - 7, SIDE), -1, I32)], axis=0
    )
    turned = stacked.T
    places = [jnp.broadcast_to(turned[:, g:g + 1], (SIDE, SIDE)) for g in range(7)]
    slot_id = lax.broadcasted_iota(I32, (SIDE, SIDE), 0)
    lane_id = lax.broadcasted_iota(I32, (SIDE, SIDE), 1)
    slot_v[...] = jnp.full(slot_v.shape, slots, I32)

    def find(b, carry):
        best = jnp.full((SIDE, SIDE), slots, I32)
        for g in range(7):
            best = jnp.where(places[g] == lane_id + b * SIDE, slot_id + g * SIDE, best)
        slot_v[pl.ds(b, 1), :] = jnp.min(best, axis=0, keepdims=True)
        return carry

    lax.fori_loop(0, row_tiles * 32 // SIDE, find, 0)
    to_scalar = pltpu.make_async_copy(slot_v, slot_s, local_sem.at[4])
    to_scalar.start()


    lax.fori_loop(12, late // CHUNK, slot_sums, 0)
    own = column_sums(0, late)
    lax.fori_loop(late // CHUNK, chunks, slot_sums, 0)
    own = own + column_sums(late, slots)

    pl.semaphore_wait(y_two, 1)
    tell(z_two, z_other)

    colx[row] = own
    colx_copies = [
        send(colx.at[row], colx.at[row], colx_send.at[i], colx_recv.at[i], device)
        for i, device in enumerate(row_peers)
    ]
    for copy in colx_copies:
        copy.start()
    for copy in feat_copies:
        copy.wait_recv()

    def project(j, carry):
        projected[pl.ds(pl.multiple_of(j * group, group), group), :] = jnp.dot(
            feats[j], weight[...], preferred_element_type=F32
        )
        return carry

    lax.fori_loop(0, n_row, project, 0)
    to_scalar.wait()
    for copy in colx_copies:
        copy.wait_recv()
    degree = colx[0]
    for j in range(1, n_row):
        degree = degree + colx[j]
    factor = lax.rsqrt(1.0 + degree)
    factor = jnp.concatenate([factor, jnp.ones((SIDE - col_tiles, SIDE), F32)], axis=0).T
    for c in range(col_tiles):
        block = projected[c * SIDE:(c + 1) * SIDE, :] * factor[:, c:c + 1]
        scaled[c * SIDE:(c + 1) * SIDE, :SIDE] = block.astype(BF16)

    pl.semaphore_wait(z_one, 1)
    pl.semaphore_wait(z_two, 1)

    eye = jnp.where(slot_id == lane_id, 1.0, 0.0)

    def sib_copy(k):
        return send(full.at[k, 1 - core], sib.at[k], sib_send.at[k], sib_recv.at[k], sibling)

    def step_peer(k):
        return chip_peer(table(k, [d[0] for d in ORDER]), table(k, [d[1] for d in ORDER]))

    def owner_copy(k, device):
        return send(full.at[k, core], land.at[k], own_send.at[k], own_recv.at[k], device)

    def pair_sum(k):
        sib_copy(k).wait_recv()
        return full[k, core].astype(F32) + sib[k].astype(F32)

    def pass_on(k):
        total = pair_sum(k)
        full[k, core, pl.ds(0, group), :] = total[:group].astype(BF16)
        full[k, core, pl.ds(group, EXTRA), :] = split_sums(join_sums(total[group:]))
        owner_copy(k, step_peer(k)).start()

    def product(k, carry):
        first = (step_peer(k)[1] // 2) * step_tiles
        wide = []
        for a in range(step_tiles):
            at_row = first + a
            wide.append(jnp.concatenate(
                [tiles[slot_s[at_row // 4, (at_row % 4) * 32 + c]] for c in range(col_tiles)], axis=1
            ))
        result = jnp.dot(jnp.concatenate(wide, axis=0), scaled[...], preferred_element_type=F32)
        for h in range(2):
            part = result[h * group:(h + 1) * group]
            full[k, h, pl.ds(0, group), :] = part[:, :SIDE].astype(BF16)
            sums = [
                jnp.sum(part[i * SIDE:(i + 1) * SIDE, SIDE:] * eye, axis=0, keepdims=True)
                for i in range(owner_tiles)
            ]
            sums.append(jnp.zeros((8 - owner_tiles, SIDE), F32))
            full[k, h, pl.ds(group, EXTRA), :] = split_sums(jnp.concatenate(sums, axis=0))
        sib_copy(k).start()

        @pl.when(k > 0)
        def _():
            pass_on(k - 1)

        return carry

    lax.fori_loop(0, 8, product, 0)

    last = len(ORDER) - 1
    total = pair_sum(last)
    for k in range(last):
        owner_copy(k, owners[k]).wait_recv()
        total = total + land[k].astype(F32)
    norm = lax.rsqrt(1.0 + join_sums(total[group:]))
    norm = jnp.concatenate([norm, jnp.ones((SIDE - 8, SIDE), F32)], axis=0).T
    for i in range(owner_tiles):
        out_ref[i * SIDE:(i + 1) * SIDE, :] = (total[i * SIDE:(i + 1) * SIDE] * norm[:, i:i + 1]).astype(BF16)

    for copy in feat_copies + colx_copies:
        copy.wait_send()
    for k in range(len(ORDER)):
        sib_copy(k).wait_send()
    for k in range(last):
        owner_copy(k, owners[k]).wait_send()


def body(features, weight, tiles, tile_rows, tile_cols, tile_count):
    n_row, n_col = lax.axis_size("row"), lax.axis_size("col")
    group, width = features.shape
    hidden = weight.shape[1]
    slots, side = tiles.shape[2], tiles.shape[3]
    row_tiles = n_col * group // side
    col_tiles = n_row * group // side
    block = group + EXTRA
    dma = pltpu.SemaphoreType.DMA

    def run(*refs):
        kernel(n_row, n_col, slots, row_tiles, col_tiles, *refs)

    anywhere = pl.BlockSpec(memory_space=pl.ANY)
    return pl.pallas_call(
        run,
        out_shape=pltpu.VMEM((group, hidden), BF16),
        in_specs=[anywhere] * 5 + [pl.BlockSpec(memory_space=pltpu.HBM)],
        out_specs=pl.BlockSpec(memory_space=pltpu.VMEM),
        scratch_shapes=[
            pltpu.VMEM((slots + 1, side, side), BF16),
            pltpu.VMEM((slots, side), F32),
            pltpu.SMEM((1, 1), I32),
            pltpu.VMEM((n_row, group, width), BF16),
            pltpu.VMEM((width, hidden), BF16),
            pltpu.VMEM((col_tiles * side, hidden), F32),
            pltpu.VMEM((col_tiles * side, 2 * hidden), BF16),
            pltpu.VMEM((1, slots), I32),
            pltpu.VMEM((1, slots), I32),
            pltpu.VMEM((16, side), I32),
            pltpu.SMEM((16, side), I32),
            pltpu.VMEM((n_row, col_tiles, side), F32),
            pltpu.VMEM((8, 2, block, hidden), BF16),
            pltpu.VMEM((8, block, hidden), BF16),
            pltpu.VMEM((7, block, hidden), BF16),
            dma((slots // CHUNK,)),
            dma((6,)),
            dma((n_row - 1,)),
            dma((n_row - 1,)),
            dma((n_row - 1,)),
            dma((n_row - 1,)),
            dma((8,)),
            dma((8,)),
            dma((7,)),
            dma((7,)),
            pltpu.SemaphoreType.REGULAR,
            pltpu.SemaphoreType.REGULAR,
            pltpu.SemaphoreType.REGULAR,
        ],
        compiler_params=pltpu.CompilerParams(
            collective_id=0, has_side_effects=True, vmem_limit_bytes=56 * 2**20
        ),
    )(
        features, weight, tiles.reshape(slots, side, side),
        tile_rows.reshape(1, slots), tile_cols.reshape(1, slots), tile_count.reshape(1, 1),
    )


def solution(mesh):
    in_specs = (
        P(("col", "row"), None),
        P(),
        P("row", "col", None, None, None),
        P("row", "col", None),
        P("row", "col", None),
        P("row", "col"),
    )
    out_specs = P(("row", "col"), None)
    return jax.shard_map(body, mesh=mesh, in_specs=in_specs, out_specs=out_specs, check_vma=False)
```

```python
import jax
import jax.numpy as jnp
from jax import lax
from jax.experimental import pallas as pl
from jax.experimental.pallas import tpu as pltpu
from jax.sharding import PartitionSpec as P

F32, BF16, I32 = jnp.float32, jnp.bfloat16, jnp.int32
SIDE = 128
CHUNK = 32
EXTRA = 16
FIRST = 3
AHEAD = 10
ORDER = ((2, 1), (0, 1), (2, 0), (1, 1), (3, 1), (1, 0), (3, 0), (0, 0))


def table(step, values):
    coef = list(values)
    for bit in (1, 2, 4):
        for i in range(8):
            if i & bit:
                coef[i] -= coef[i - bit]
    bits = (step % 2, (step // 2) % 2, step // 4)
    total = coef[0]
    for i in range(1, 8):
        if coef[i]:
            term = coef[i]
            for j in range(3):
                if i >> j & 1:
                    term = term * bits[j]
            total = total + term
    return total


def split_sums(value):
    high = value.astype(BF16)
    low = (value - high.astype(F32)).astype(BF16)
    return jnp.concatenate([high, low], axis=0)


def join_sums(value):
    return value[:8] + value[8:]


def kernel(
    n_row, n_col, slots, row_tiles, col_tiles,
    feat_hbm, weight_hbm, tiles_hbm, rows_hbm, cols_hbm, count_hbm, out_ref,
    tiles, csum, count_s, feats, weight, projected, scaled, rows_v, cols_v, slot_v, slot_s, colx,
    full, sib, land,
    tile_sem, local_sem, feat_send, feat_recv, colx_send, colx_recv, sib_send, sib_recv,
    own_send, own_recv, y_two, z_one, z_two,
):
    group = feat_hbm.shape[0]
    owner_tiles = group // SIDE
    step_tiles = 2 * owner_tiles
    row = lax.axis_index("row")
    col = lax.axis_index("col")
    core = col % 2
    z_hi = (col // 2) % 2
    y = col // 4
    sibling = (row, col + 1 - 2 * core)

    def chip_peer(dy, dz):
        return (row, (((y + dy) % 4) * 2 + (z_hi + dz) % 2) * 2 + core)

    row_peers = [((row + i) % n_row, col) for i in range(1, n_row)]

    def tile_copy(k):
        part = pl.ds(k * CHUNK, CHUNK)
        return pltpu.make_async_copy(tiles_hbm.at[part], tiles.at[part], tile_sem.at[k])

    def send(src, dst, send_sem, recv_sem, device):
        return pltpu.make_async_remote_copy(
            src_ref=src, dst_ref=dst, send_sem=send_sem, recv_sem=recv_sem,
            device_id=device, device_id_type=pl.DeviceIdType.MESH,
        )

    chunks = slots // CHUNK
    local = [
        pltpu.make_async_copy(cols_hbm, cols_v, local_sem.at[0]),
        pltpu.make_async_copy(rows_hbm, rows_v, local_sem.at[1]),
        pltpu.make_async_copy(weight_hbm, weight, local_sem.at[2]),
        pltpu.make_async_copy(feat_hbm, feats.at[row], local_sem.at[3]),
        pltpu.make_async_copy(count_hbm, count_s, local_sem.at[5]),
    ]
    for k in range(FIRST):
        tile_copy(k).start()
    for copy in local:
        copy.start()
    barrier = pltpu.get_barrier_semaphore()
    owners = [chip_peer(dy, dz) for dy, dz in ORDER[:-1]]
    y_next, y_prev, z_other = chip_peer(1, 0), chip_peer(3, 0), chip_peer(0, 1)
    partners = row_peers + [sibling, y_next, y_prev, z_other]
    for device in partners:
        pl.semaphore_signal(barrier, inc=1, device_id=device, device_id_type=pl.DeviceIdType.MESH)
    for k in range(FIRST, AHEAD):
        tile_copy(k).start()
    pl.semaphore_wait(barrier, len(partners))
    feat_copies = [
        send(feat_hbm, feats.at[row], feat_send.at[i], feat_recv.at[i], device)
        for i, device in enumerate(row_peers)
    ]
    for copy in feat_copies:
        copy.start()
    for k in range(AHEAD, chunks):
        tile_copy(k).start()

    def tell(sem, device):
        pl.semaphore_signal(sem, inc=1, device_id=device, device_id_type=pl.DeviceIdType.MESH)

    tell(y_two, y_prev)
    tell(z_one, z_other)

    tiles[slots] = jnp.zeros((SIDE, SIDE), BF16)
    scaled[:, SIDE:] = jnp.ones((col_tiles * SIDE, SIDE), BF16)
    sublane = lax.broadcasted_iota(I32, (8, SIDE), 0)

    def slot_sums(k, carry):
        tile_copy(k).wait()
        for g in range(CHUNK // 8):
            first = k * CHUNK + g * 8
            sums = None
            for s in range(8):
                tile = tiles[first + s].astype(F32)
                part = jnp.sum(tile.reshape(SIDE // 8, 8, SIDE), axis=0)
                part = jnp.broadcast_to(jnp.sum(part, axis=0, keepdims=True), (8, SIDE))
                sums = part if s == 0 else jnp.where(sublane == s, part, sums)
            csum[pl.ds(pl.multiple_of(first, 8), 8), :] = sums
        return carry

    def column_sums(first, end):
        size = end - first
        kind = lax.broadcasted_iota(I32, (col_tiles, size), 0)
        at = lax.broadcasted_iota(I32, (col_tiles, size), 1) + first
        pick = jnp.where((kind == cols_v[:, first:end]) & (at < count), 1.0, 0.0).astype(BF16)
        live = lax.broadcasted_iota(I32, (size, SIDE), 0) + first < count
        rest = jnp.where(live, csum[first:end], 0.0)
        total = jnp.zeros((col_tiles, SIDE), F32)
        for _ in range(3):
            piece = rest.astype(BF16)
            total = total + jnp.dot(pick, piece, preferred_element_type=F32)
            rest = rest - piece.astype(F32)
        return total

    late = (slots - 1) // SIDE * SIDE
    lax.fori_loop(0, 12, slot_sums, 0)

    for copy in local:
        copy.wait()
    count = count_s[0, 0]
    lane = lax.broadcasted_iota(I32, (1, slots), 1)
    place = jnp.where(lane < count, rows_v[...] * 32 + cols_v[...], -1)
    padded = jnp.concatenate([place, jnp.full((1, 7 * SIDE - slots), -1, I32)], axis=1)
    stacked = jnp.concatenate(
        [padded[:, g * SIDE:(g + 1) * SIDE] for g in range(7)] + [jnp.full((SIDE - 7, SIDE), -1, I32)], axis=0
    )
    turned = stacked.T
    places = [jnp.broadcast_to(turned[:, g:g + 1], (SIDE, SIDE)) for g in range(7)]
    slot_id = lax.broadcasted_iota(I32, (SIDE, SIDE), 0)
    lane_id = lax.broadcasted_iota(I32, (SIDE, SIDE), 1)
    slot_v[...] = jnp.full(slot_v.shape, slots, I32)

    def find(b, carry):
        best = jnp.full((SIDE, SIDE), slots, I32)
        for g in range(7):
            best = jnp.where(places[g] == lane_id + b * SIDE, slot_id + g * SIDE, best)
        slot_v[pl.ds(b, 1), :] = jnp.min(best, axis=0, keepdims=True)
        return carry

    lax.fori_loop(0, row_tiles * 32 // SIDE, find, 0)
    to_scalar = pltpu.make_async_copy(slot_v, slot_s, local_sem.at[4])
    to_scalar.start()


    lax.fori_loop(12, late // CHUNK, slot_sums, 0)
    own = column_sums(0, late)
    lax.fori_loop(late // CHUNK, chunks, slot_sums, 0)
    own = own + column_sums(late, slots)

    pl.semaphore_wait(y_two, 1)
    tell(z_two, z_other)

    colx[row] = own
    colx_copies = [
        send(colx.at[row], colx.at[row], colx_send.at[i], colx_recv.at[i], device)
        for i, device in enumerate(row_peers)
    ]
    for copy in colx_copies:
        copy.start()
    for copy in feat_copies:
        copy.wait_recv()

    def project(j, carry):
        projected[pl.ds(pl.multiple_of(j * group, group), group), :] = jnp.dot(
            feats[j], weight[...], preferred_element_type=F32
        )
        return carry

    lax.fori_loop(0, n_row, project, 0)
    to_scalar.wait()
    for copy in colx_copies:
        copy.wait_recv()
    degree = colx[0]
    for j in range(1, n_row):
        degree = degree + colx[j]
    factor = lax.rsqrt(1.0 + degree)
    factor = jnp.concatenate([factor, jnp.ones((SIDE - col_tiles, SIDE), F32)], axis=0).T
    for c in range(col_tiles):
        block = projected[c * SIDE:(c + 1) * SIDE, :] * factor[:, c:c + 1]
        scaled[c * SIDE:(c + 1) * SIDE, :SIDE] = block.astype(BF16)

    pl.semaphore_wait(z_one, 1)
    pl.semaphore_wait(z_two, 1)

    eye = jnp.where(slot_id == lane_id, 1.0, 0.0)

    def sib_copy(k):
        return send(full.at[k, 1 - core], sib.at[k], sib_send.at[k], sib_recv.at[k], sibling)

    def step_peer(k):
        return chip_peer(table(k, [d[0] for d in ORDER]), table(k, [d[1] for d in ORDER]))

    def owner_copy(k, device):
        return send(full.at[k, core], land.at[k], own_send.at[k], own_recv.at[k], device)

    def pair_sum(k):
        sib_copy(k).wait_recv()
        return full[k, core].astype(F32) + sib[k].astype(F32)

    def pass_on(k):
        total = pair_sum(k)
        full[k, core, pl.ds(0, group), :] = total[:group].astype(BF16)
        full[k, core, pl.ds(group, EXTRA), :] = split_sums(join_sums(total[group:]))
        owner_copy(k, step_peer(k)).start()

    def product(k, carry):
        first = (step_peer(k)[1] // 2) * step_tiles
        wide = []
        for a in range(step_tiles):
            at_row = first + a
            wide.append(jnp.concatenate(
                [tiles[slot_s[at_row // 4, (at_row % 4) * 32 + c]] for c in range(col_tiles)], axis=1
            ))
        result = jnp.dot(jnp.concatenate(wide, axis=0), scaled[...], preferred_element_type=F32)
        for h in range(2):
            part = result[h * group:(h + 1) * group]
            full[k, h, pl.ds(0, group), :] = part[:, :SIDE].astype(BF16)
            sums = [
                jnp.sum(part[i * SIDE:(i + 1) * SIDE, SIDE:] * eye, axis=0, keepdims=True)
                for i in range(owner_tiles)
            ]
            sums.append(jnp.zeros((8 - owner_tiles, SIDE), F32))
            full[k, h, pl.ds(group, EXTRA), :] = split_sums(jnp.concatenate(sums, axis=0))
        sib_copy(k).start()

        @pl.when(k > 0)
        def _():
            pass_on(k - 1)

        return carry

    lax.fori_loop(0, 8, product, 0)

    last = len(ORDER) - 1
    sum_rows = pl.ds(0, group + EXTRA)
    projected[sum_rows, :] = pair_sum(last)

    def collect(k, carry):
        owner_copy(k, step_peer(k)).wait_recv()
        projected[sum_rows, :] += land[k].astype(F32)
        return carry

    lax.fori_loop(0, last, collect, 0)
    total = projected[sum_rows, :]
    norm = lax.rsqrt(1.0 + join_sums(total[group:]))
    norm = jnp.concatenate([norm, jnp.ones((SIDE - 8, SIDE), F32)], axis=0).T
    for i in range(owner_tiles):
        out_ref[i * SIDE:(i + 1) * SIDE, :] = (total[i * SIDE:(i + 1) * SIDE] * norm[:, i:i + 1]).astype(BF16)

    for copy in feat_copies + colx_copies:
        copy.wait_send()
    for k in range(len(ORDER)):
        sib_copy(k).wait_send()
    for k in range(last):
        owner_copy(k, owners[k]).wait_send()


def body(features, weight, tiles, tile_rows, tile_cols, tile_count):
    n_row, n_col = lax.axis_size("row"), lax.axis_size("col")
    group, width = features.shape
    hidden = weight.shape[1]
    slots, side = tiles.shape[2], tiles.shape[3]
    row_tiles = n_col * group // side
    col_tiles = n_row * group // side
    block = group + EXTRA
    dma = pltpu.SemaphoreType.DMA

    def run(*refs):
        kernel(n_row, n_col, slots, row_tiles, col_tiles, *refs)

    anywhere = pl.BlockSpec(memory_space=pl.ANY)
    return pl.pallas_call(
        run,
        out_shape=pltpu.VMEM((group, hidden), BF16),
        in_specs=[anywhere] * 5 + [pl.BlockSpec(memory_space=pltpu.HBM)],
        out_specs=pl.BlockSpec(memory_space=pltpu.VMEM),
        scratch_shapes=[
            pltpu.VMEM((slots + 1, side, side), BF16),
            pltpu.VMEM((slots, side), F32),
            pltpu.SMEM((1, 1), I32),
            pltpu.VMEM((n_row, group, width), BF16),
            pltpu.VMEM((width, hidden), BF16),
            pltpu.VMEM((col_tiles * side, hidden), F32),
            pltpu.VMEM((col_tiles * side, 2 * hidden), BF16),
            pltpu.VMEM((1, slots), I32),
            pltpu.VMEM((1, slots), I32),
            pltpu.VMEM((16, side), I32),
            pltpu.SMEM((16, side), I32),
            pltpu.VMEM((n_row, col_tiles, side), F32),
            pltpu.VMEM((8, 2, block, hidden), BF16),
            pltpu.VMEM((8, block, hidden), BF16),
            pltpu.VMEM((7, block, hidden), BF16),
            dma((slots // CHUNK,)),
            dma((6,)),
            dma((n_row - 1,)),
            dma((n_row - 1,)),
            dma((n_row - 1,)),
            dma((n_row - 1,)),
            dma((8,)),
            dma((8,)),
            dma((7,)),
            dma((7,)),
            pltpu.SemaphoreType.REGULAR,
            pltpu.SemaphoreType.REGULAR,
            pltpu.SemaphoreType.REGULAR,
        ],
        compiler_params=pltpu.CompilerParams(
            collective_id=0, has_side_effects=True, vmem_limit_bytes=56 * 2**20
        ),
    )(
        features, weight, tiles.reshape(slots, side, side),
        tile_rows.reshape(1, slots), tile_cols.reshape(1, slots), tile_count.reshape(1, 1),
    )


def solution(mesh):
    in_specs = (
        P(("col", "row"), None),
        P(),
        P("row", "col", None, None, None),
        P("row", "col", None),
        P("row", "col", None),
        P("row", "col"),
    )
    out_specs = P(("row", "col"), None)
    return jax.shard_map(body, mesh=mesh, in_specs=in_specs, out_specs=out_specs, check_vma=False)
```
